32 devices in a mesh: groups: 1, ep: 32 (over z, y, x, core).
Axes of the slice: x: 2, y: 2, z: 4, core: 2. Of those that a mesh axis runs over, the one named last changes fastest.
Arguments:
- hidden: bfloat16 [256, 7168], P(('groups', 'ep')), may hold values from -6 to 6
- queries: bfloat16 [256, 128, 576], P(('groups', 'ep')), may hold values from -6 to 6
- cache: bfloat16 [256, 256, 576], P(('groups', 'ep')), may hold values from -6 to 6
- lengths: int32 [256], P(('groups', 'ep')), may hold values from 1 to 256, 32768 in all
- value_up: bfloat16 [128, 512, 128], P('ep'), may hold values from -0.25 to 0.25
- out_proj: bfloat16 [16384, 7168], P('ep'), may hold values from -0.09375 to 0.09375
- norm_gain: bfloat16 [7168], replicated, may hold values from 0.25 to 1.75
- routes: int32 [256, 2], P(('groups', 'ep')), may hold values from 0 to 3, all different within a row; in each aligned block of 8 rows (0 to 7, 8 to 15, ...) at most 8 rows name the same one
- gates: float32 [256, 2], P(('groups', 'ep')), may hold values from 0.3 to 1.5
- expert_slot: int32 [4], replicated, may hold values from 0 to 3, each once
- w_gate: bfloat16 [7168, 4096], P(None, 'ep'), may hold values from -0.0625 to 0.0625
- w_up: bfloat16 [7168, 4096], P(None, 'ep'), may hold values from -0.0625 to 0.0625
- w_down: bfloat16 [4096, 7168], P('ep'), may hold values from -0.1875 to 0.1875
Outputs:
- result: bfloat16 [256, 7168], P(('groups', 'ep'))
The draws below stay inside these ranges and needn't reach their ends.
Inputs may be any that keep to these rules, and one draw needn't show every extreme that they name: `routes`: each row names 2 different logical experts. Among the rows of one device no expert is named by more than 8 rows, a bound that some block reaches of them. `expert_slot`: each slot appears once. `lengths`: the largest length is exactly 256.
All inputs are finite; a program needn't handle non-finite values. No bound on the sum of `lengths` on one device may be relied on, other than what follows from the above.
Results may differ from the reference program's by a relative error of at most 0.0065.
Values may be sent and summed in bfloat16 or wider, within the bound.
No kernel may reach another device: no remote copies, remote signals or barrier semaphores. Data moves between devices by JAX's collectives and lax.ppermute only.
A program may use at most 128 MiB of HBM per device.

```python
import math
import jax
import jax.numpy as jnp
import numpy as np
from jax import lax

D = 7168
HEADS = 128
LATENT = 512
ROPE = 64
VDIM = 128
HID_DEV = 128
SLABS = 8
ROUTES = 2
REQ_DEV = 8
CTX = 256
FFH = 1024
EXPERTS = 4
BATCH = 256
CAP = 8
N_EP = 32


def draw_queries(key, part):
    key = jax.random.fold_in(key, 31)
    noise_key = jax.random.fold_in(key, 0)
    array_shape = (BATCH, HEADS, LATENT + ROPE)
    entries = jnp.clip(jax.random.normal(noise_key, array_shape, jnp.float32), -6.0, 6.0)
    return entries.astype(jnp.bfloat16)


def draw_cache(key, part):
    key = jax.random.fold_in(key, 47)
    array_shape = (BATCH, CTX, LATENT + ROPE)
    entries = jnp.clip(jax.random.normal(key, array_shape, jnp.float32), -6.0, 6.0)
    return entries.astype(jnp.bfloat16)


def steps_of(own_key, dims, pieces, least, high):
    def one(position, parts):
        heights = jax.random.uniform(jax.random.fold_in(jax.random.fold_in(own_key, 6), position), (parts,), jnp.float32, least / len(pieces), high / len(pieces))
        return jnp.repeat(jnp.exp(heights), dims[position] // parts).reshape((-1,) + (1,) * (len(dims) - position - 1))

    gain = one(*pieces[0])
    for cut in pieces[1:]:
        gain = gain * one(*cut)
    return gain


def length_profile(count, total, bound, slope):
    portions = [(1 << 20) // math.isqrt(grade ** slope) + 1 for grade in range(2, count + 1)]
    spare, given = total - bound - (count - 1), [1] * (count - 1)
    while spare > 0:
        movable = [i for i in range(count - 1) if given[i] < bound]
        pool, budget = sum([portions[i] for i in movable]), spare
        for i in movable:
            more = min(bound - given[i], max(1, budget * portions[i] // pool), spare)
            given[i] = given[i] + more
            spare = spare - more
    return np.array([bound] + given)


def uneven(stream_key, number_of, total, limit, lean):
    if number_of == 2:
        one = jax.random.randint(stream_key, (), max(1, total - limit), min(limit, total - 1) + 1)
        return jnp.stack([one, total - one])
    tallies = jnp.asarray(length_profile(number_of, total, limit, lean), jnp.int32)
    couples = (number_of - 1) // 2
    source_of, receiver = tallies[1:1 + 2 * couples:2], tallies[2:2 + 2 * couples:2]
    room = jnp.minimum(source_of - 1, limit - receiver)
    shifted = jax.random.randint(jax.random.fold_in(stream_key, 1), (couples,), 0, 1 << 20) % (room + 1)
    tallies = tallies.at[1:1 + 2 * couples:2].set(source_of - shifted).at[2:2 + 2 * couples:2].set(receiver + shifted)
    return tallies[jax.random.permutation(jax.random.fold_in(stream_key, 2), number_of)]


def routed_block(own_key, own, number, rows, number_of, top, bound, skew):
    sequence = jax.random.permutation(own_key, number_of)
    packed, common = load_shares(number_of, rows * top, bound, skew, True), load_shares(number_of, rows * top, bound, skew, False)
    places = jnp.arange(number_of)

    def named(sizes, turn):
        used = int((sizes > 0).sum())
        fixed = max(1, used // 4)
        passed = fixed + (places - fixed + turn * (used - fixed)) % max(1, number_of - fixed)
        return jnp.zeros((number_of,), jnp.int32).at[sequence[jnp.where(places < fixed, places, passed)]].set(jnp.asarray(sizes, jnp.int32))

    sizes = jnp.where(number % 4 == 0, named(packed, number // 4), named(common, number - number // 4 - 1))
    mixed = jax.random.permutation(jax.random.fold_in(own, 3), number_of)
    source_of, receiver = mixed[0:number_of // 2 * 2:2], mixed[1:number_of // 2 * 2:2]
    slack = jnp.minimum(sizes[source_of] - 1, bound - sizes[receiver]) // 2
    slack = jnp.where((source_of == sequence[0]) | (receiver == sequence[0]) | (sizes[receiver] == 0), 0, jnp.maximum(slack, 0))
    passed = jax.random.randint(jax.random.fold_in(own, 4), (number_of // 2,), 0, 1 << 20) % (slack + 1)
    sizes = sizes.at[source_of].add(-passed).at[receiver].add(passed)
    items = jnp.searchsorted(jnp.cumsum(sizes), jnp.arange(rows * top), side="right").astype(jnp.int32)
    table = items.reshape(top, rows).T
    table = table[jax.random.permutation(jax.random.fold_in(own, 1), rows)]
    turn = jax.random.randint(jax.random.fold_in(own, 2), (rows, 1), 0, top)
    return jnp.take_along_axis(table, (jnp.arange(top)[None, :] + turn) % top, axis=1)


def load_shares(amount, total, limit, skew, full):
    portions = [(1 << 20) // math.isqrt(standing ** skew) + 1 for standing in range(1, amount + 1)]
    largest = limit if full else min(limit, max(-(-total // amount), total * portions[0] // sum(portions)))
    least = 1 if total - largest >= amount - 1 else 0
    holding, surplus = [largest] + [least] * (amount - 1), total - largest - least * (amount - 1)
    while surplus > 0:
        candidates = [i for i in range(1, amount) if holding[i] < largest] or [i for i in range(1, amount) if holding[i] < limit]
        whole, remaining = sum([portions[i] for i in candidates]), surplus
        for i in candidates:
            extra = min(limit - holding[i], max(1, remaining * portions[i] // whole), surplus)
            holding[i] = holding[i] + extra
            surplus = surplus - extra
    return np.array(holding)


def centred(key, extent, deviation, limit, shards=(), kind=jnp.bfloat16):
    result = deviation * jax.random.normal(key, extent, jnp.float32)
    if shards:
        result = result * steps_of(key, extent, shards, -0.22, 0.18)
    return jnp.clip(result, -limit, limit).astype(kind)


def setup_inputs(seed: int = 0, part: int = 0) -> dict:
    streams_of = jax.random.split(jax.random.key(seed), 14)
    part_splits = jax.random.split(jax.random.fold_in(streams_of[13], part), 14)
    hidden = centred(part_splits[0], (BATCH, D), 1.0, 6.0, ((0, 32),))
    queries = draw_queries(jax.random.fold_in(jax.random.fold_in(streams_of[13], part), 71), part)
    cache = draw_cache(jax.random.fold_in(jax.random.fold_in(streams_of[13], part), 71), part)
    lengths = uneven(part_splits[3], BATCH, BATCH * CTX // 2, CTX, 2).astype(jnp.int32)
    value_up = centred(streams_of[4], (HEADS, LATENT, VDIM), LATENT ** -0.5, 0.25, ((0, 32),))
    out_proj = centred(streams_of[5], (HEADS * VDIM, D), (2.0 * (HEADS * VDIM) ** -0.5), 0.09375, ((0, 32),))
    norm_gain = jnp.clip(1.0 + 0.15 * jax.random.normal(streams_of[6], (D,), jnp.float32), 0.25, 1.75).astype(jnp.bfloat16)
    routes_keys = jax.random.split(jax.random.fold_in(part_splits[7], 1), BATCH // REQ_DEV)
    routes_turns = jax.random.permutation(jax.random.fold_in(part_splits[7], 3), BATCH // REQ_DEV)
    routes = jax.vmap(lambda own, number: routed_block(jax.random.fold_in(part_splits[7], 2), own, number, REQ_DEV, EXPERTS, ROUTES, CAP, 2))(routes_keys, routes_turns).reshape((BATCH, ROUTES))
    gates = jnp.clip(0.3 + 1.2 * jax.random.uniform(part_splits[8], (BATCH, ROUTES), jnp.float32) ** steps_of(part_splits[8], (BATCH, ROUTES), ((0, 32),), -0.2, 0.2), 0.3, 1.5)
    expert_slot = jax.random.permutation(streams_of[9], EXPERTS).astype(jnp.int32)
    w_gate = centred(streams_of[10], (D, EXPERTS * FFH), D ** -0.5, 0.0625, ((1, 32),))
    w_up = centred(streams_of[11], (D, EXPERTS * FFH), D ** -0.5, 0.0625, ((1, 32),))
    w_down = centred(streams_of[12], (EXPERTS * FFH, D), FFH ** -0.5, 0.1875, ((0, 32),))
    return dict(hidden=hidden, queries=queries, cache=cache, lengths=lengths, value_up=value_up, out_proj=out_proj, norm_gain=norm_gain, routes=routes, gates=gates, expert_slot=expert_slot, w_gate=w_gate, w_up=w_up, w_down=w_down)


score_scale = 192.0 ** (-0.5)
norm_eps = 1e-06

def attend_one(request):
    query_rows, cache_rows, length = request
    scores = jnp.dot(query_rows, cache_rows.T, preferred_element_type=jnp.float32) * score_scale
    live_mask = jnp.arange(CTX, dtype=jnp.int32)[None, :] < length
    row_max = lax.optimization_barrier(jnp.max(jnp.where(live_mask, scores, -jnp.inf), axis=1, keepdims=True))
    raised = jnp.where(live_mask, jnp.exp(scores - row_max), 0.0)
    probs_bf = (raised / lax.optimization_barrier(jnp.sum(raised, axis=1, keepdims=True))).astype(jnp.bfloat16)
    return jnp.dot(probs_bf, cache_rows[:, :LATENT], preferred_element_type=jnp.float32).astype(jnp.bfloat16)

def reference(hidden, queries, cache, lengths, value_up, out_proj, norm_gain, routes, gates, expert_slot, w_gate, w_up, w_down):
    latent_out = lax.map(attend_one, (queries, cache, lengths))
    head_values = jnp.einsum('bhl,hlv->bhv', latent_out.astype(jnp.float32), value_up.astype(jnp.float32), precision=lax.Precision.HIGHEST).astype(jnp.bfloat16)
    attended = jnp.dot(head_values.reshape(BATCH, HEADS * VDIM), out_proj, preferred_element_type=jnp.float32)
    mixed = hidden.astype(jnp.float32) + attended
    normed = (mixed / jnp.sqrt(lax.optimization_barrier(jnp.mean(mixed * mixed, axis=1, keepdims=True)) + norm_eps) * norm_gain.astype(jnp.float32)).astype(jnp.bfloat16)
    physical = expert_slot[routes]
    row_limit = N_EP * CAP

    def add_expert(slot_id, total):
        route_hit = physical == slot_id
        token_hit = jnp.any(route_hit, axis=1)
        token_gate = lax.optimization_barrier(jnp.sum(jnp.where(route_hit, gates, 0.0), axis=1))
        row_ids = jnp.nonzero(token_hit, size=row_limit, fill_value=0)[0]
        valid = jnp.arange(row_limit) < jnp.sum(token_hit.astype(jnp.int32))
        chosen_rows = normed[row_ids]
        start = (slot_id * FFH).astype(jnp.int32)
        gate_cols = lax.dynamic_slice_in_dim(w_gate, start, FFH, 1)
        up_cols = lax.dynamic_slice_in_dim(w_up, start, FFH, 1)
        down_rows = lax.dynamic_slice_in_dim(w_down, start, FFH, 0)
        gate_act = jnp.dot(chosen_rows, gate_cols, preferred_element_type=jnp.float32)
        up_act = jnp.dot(chosen_rows, up_cols, preferred_element_type=jnp.float32)
        inner_act = (jax.nn.silu(gate_act) * up_act).astype(jnp.bfloat16)
        slab_parts = jnp.einsum('rsh,shd->srd', inner_act.reshape(row_limit, SLABS, HID_DEV).astype(jnp.float32), down_rows.reshape(SLABS, HID_DEV, D).astype(jnp.float32), precision=lax.Precision.HIGHEST).astype(jnp.bfloat16)
        expert_out = lax.optimization_barrier(jnp.sum(slab_parts.astype(jnp.float32), axis=0))
        weight = jnp.where(valid, token_gate[row_ids], 0.0)
        return total.at[row_ids].add(expert_out * weight[:, None])
    moe = lax.fori_loop(0, EXPERTS, add_expert, jnp.zeros((BATCH, D), jnp.float32))
    return (mixed + moe).astype(jnp.bfloat16)
```

```python
import jax
import jax.numpy as jnp
import numpy as np
from jax import lax
from jax.sharding import PartitionSpec as P

LATENT = 512
SLABS = 8
F32 = jnp.float32
BF16 = jnp.bfloat16

score_scale = 192.0 ** (-0.5)
norm_eps = 1e-06

CORE, AX, AY = 1, 2, 4


def attend(queries, cache, lengths):
    scores = jnp.einsum("bhr,bpr->bhp", queries, cache, preferred_element_type=F32) * score_scale
    live_mask = lax.broadcasted_iota(jnp.int32, scores.shape, 2) < lengths[:, None, None]
    row_max = jnp.max(jnp.where(live_mask, scores, -jnp.inf), axis=2, keepdims=True)
    raised = jnp.where(live_mask, jnp.exp(scores - row_max), 0.0)
    probs_bf = (raised / jnp.sum(raised, axis=2, keepdims=True)).astype(BF16)
    return jnp.einsum(
        "bhp,bpl->bhl", probs_bf, cache[:, :, :LATENT], preferred_element_type=F32
    ).astype(BF16)


def relative_order(first, second, planes):
    return np.array(
        [
            z * SLABS + b * second + a * first + c
            for c in (0, 1)
            for a in (0, 1)
            for b in (0, 1)
            for z in range(planes)
        ],
        np.int32,
    )


def on_device(devices):
    planes = devices // SLABS

    def swap(x, mask):
        return lax.ppermute(x, "ep", [(i, i ^ mask) for i in range(devices)])

    def halve(x, mask):
        half = x.shape[0] // 2
        return x[:half] + swap(x[half:].astype(BF16), mask).astype(F32)

    def sum_to_owner(product, rows):
        outs = []
        sent = [swap(product(g, 1).astype(BF16), CORE) for g in (0, 1)]
        for g, (first, second) in enumerate(((AX, AY), (AY, AX))):
            x = product(g, 0) + sent[g].astype(F32)
            x = halve(x, first)
            outs.append(halve(x, second))
        x = jnp.concatenate(outs, axis=1)
        total = x[:rows]
        for d in range(1, planes):
            total = total + swap(x[d * rows : (d + 1) * rows].astype(BF16), d * SLABS).astype(F32)
        return total

    def to_all(x, cut):
        x = jnp.concatenate([x] + [swap(x, d * SLABS) for d in range(1, planes)], axis=0)
        groups = []
        for part, (first, second) in zip((x[:, :cut], x[:, cut:]), ((AX, AY), (AY, AX))):
            for mask in (second, first, CORE):
                part = jnp.concatenate([part, swap(part, mask)], axis=0)
            groups.append(part)
        return groups

    def body(
        hidden, queries, cache, lengths, value_up, out_proj, norm_gain,
        routes, gates, expert_slot, w_gate, w_up, w_down,
    ):
        rows, width = hidden.shape
        half = width // 2
        me = lax.axis_index("ep")
        orders = [relative_order(AX, AY, planes), relative_order(AY, AX, planes)]
        experts = expert_slot.shape[0]
        labels = jnp.arange(experts, dtype=jnp.int32)
        physical = jnp.sum(
            jnp.where(routes[:, :, None] == labels, expert_slot[None, None, :], 0), axis=2
        )
        weights = jnp.sum(
            jnp.where(physical[:, :, None] == labels, gates[:, :, None], 0.0), axis=1
        )
        pieces = []
        for _ in range(3):
            piece = lax.reduce_precision(weights, 8, 7)
            pieces.append(piece.astype(BF16))
            weights = weights - piece
        tail = jnp.pad(jnp.concatenate(pieces, axis=1), ((0, 0), (0, 128 - 3 * experts)))
        places = [jnp.bitwise_xor(jnp.asarray(order), me) for order in orders]

        latent_out = attend(queries, cache, lengths)
        by_heads = lax.all_to_all(latent_out, "ep", split_axis=1, concat_axis=0, tiled=True)
        head_values = jnp.einsum(
            "bhl,hlv->bhv", by_heads, value_up, preferred_element_type=F32
        ).astype(BF16)
        flat_values = head_values.reshape(head_values.shape[0], -1)
        total_rows = flat_values.shape[0]
        picks = []
        for place in places:
            wanted = (place[:, None] * rows + jnp.arange(rows, dtype=jnp.int32)).reshape(-1, 1)
            pick = (wanted == jnp.arange(total_rows, dtype=jnp.int32)[None, :]).astype(BF16)
            picks.append(jnp.dot(pick, flat_values, preferred_element_type=F32).astype(BF16))
        cut = total_rows // 2

        def out_part(g, part):
            return jnp.dot(
                picks[g][part * cut : (part + 1) * cut],
                out_proj[:, g * half : (g + 1) * half],
                preferred_element_type=F32,
            )

        mixed = hidden.astype(F32) + sum_to_owner(out_part, rows)
        scale_rows = lax.rsqrt(jnp.mean(mixed * mixed, axis=1, keepdims=True) + norm_eps)
        normed = (mixed * scale_rows * norm_gain.astype(F32)).astype(BF16)

        tokens = to_all(jnp.concatenate([normed, tail], axis=1), half)
        tails = tokens[1][:, half : half + 3 * experts].astype(F32)
        tokens = [tokens[0], tokens[1][:, :half]]

        def turn(x):
            return x.reshape(2, 2, 2, planes * rows, -1).swapaxes(1, 2).reshape(total_rows, -1)

        def act(w):
            a, b = (
                jnp.dot(tokens[g], w[g * half : (g + 1) * half], preferred_element_type=F32)
                for g in (0, 1)
            )
            return a + turn(b)

        mine = lax.broadcasted_iota(jnp.int32, tails.shape, 1) % experts == me // SLABS
        weight_b = jnp.sum(jnp.where(mine, tails, 0.0), axis=1, keepdims=True)
        weight_rows = [turn(weight_b), weight_b]
        inner = (jax.nn.silu(act(w_gate)) * act(w_up)).astype(BF16)
        inners = [inner, turn(inner)]

        def down_part(g, part):
            span = slice(part * cut, (part + 1) * cut)
            return weight_rows[g][span] * jnp.dot(
                inners[g][span], w_down[:, g * half : (g + 1) * half], preferred_element_type=F32
            )

        return (mixed + sum_to_owner(down_part, rows)).astype(BF16)

    return body


def solution(mesh):
    placed = (
        P(("groups", "ep"), None),
        P(("groups", "ep"), None, None),
        P(("groups", "ep"), None, None),
        P(("groups", "ep")),
        P("ep", None, None),
        P("ep", None),
        P(),
        P(("groups", "ep"), None),
        P(("groups", "ep"), None),
        P(),
        P(None, "ep"),
        P(None, "ep"),
        P("ep", None),
    )
    return jax.shard_map(
        on_device(mesh.shape["ep"]),
        mesh=mesh,
        in_specs=placed,
        out_specs=P(("groups", "ep"), None),
        check_vma=False,
    )
```

```python
import jax
import jax.numpy as jnp
import numpy as np
from jax import lax
from jax.sharding import PartitionSpec as P

LATENT = 512
SLABS = 8
F32 = jnp.float32
BF16 = jnp.bfloat16

score_scale = 192.0 ** (-0.5)
norm_eps = 1e-06

CORE, AX, AY = 1, 2, 4


def attend(queries, cache, lengths):
    scores = jnp.einsum("bhr,bpr->bhp", queries, cache, preferred_element_type=F32) * score_scale
    live_mask = lax.broadcasted_iota(jnp.int32, scores.shape, 2) < lengths[:, None, None]
    row_max = jnp.max(jnp.where(live_mask, scores, -jnp.inf), axis=2, keepdims=True)
    raised = jnp.where(live_mask, jnp.exp(scores - row_max), 0.0)
    probs_bf = (raised / jnp.sum(raised, axis=2, keepdims=True)).astype(BF16)
    return jnp.einsum(
        "bhp,bpl->bhl", probs_bf, cache[:, :, :LATENT], preferred_element_type=F32
    ).astype(BF16)


def relative_order(first, second, planes):
    return np.array(
        [
            z * SLABS + b * second + a * first
            for a in (0, 1)
            for b in (0, 1)
            for z in range(planes)
        ],
        np.int32,
    )


def on_device(devices):
    planes = devices // SLABS
    chips = devices // 2
    axes = ((AX, AY), (AY, AX))

    def swap(x, mask):
        return lax.ppermute(x, "ep", [(i, i ^ mask) for i in range(devices)])

    def sum_to_owner(product, rows):
        sent = [swap(product(g, 1).astype(BF16), axes[g][0]) for g in (0, 1)]
        outs = []
        for g in (0, 1):
            x = product(g, 0) + sent[g].astype(F32)
            half = x.shape[0] // 2
            outs.append(x[:half] + swap(x[half:].astype(BF16), axes[g][1]).astype(F32))
        x = jnp.concatenate(outs, axis=1)
        total = x[:rows]
        for d in range(1, planes):
            total = total + swap(x[d * rows : (d + 1) * rows].astype(BF16), d * SLABS).astype(F32)
        return total

    def to_all(x, cut):
        x = jnp.concatenate([x] + [swap(x, d * SLABS) for d in range(1, planes)], axis=0)
        near = [
            jnp.concatenate([part, swap(part, axes[g][1])], axis=0)
            for g, part in enumerate((x[:, :cut], x[:, cut:]))
        ]
        return [(near[g], swap(near[g], axes[g][0])) for g in (0, 1)]

    def body(
        hidden, queries, cache, lengths, value_up, out_proj, norm_gain,
        routes, gates, expert_slot, w_gate, w_up, w_down,
    ):
        rows, width = hidden.shape
        half = width // 2
        me = lax.axis_index("ep")
        core = me % 2
        value_up_other = swap(value_up, CORE)
        out_proj_other = swap(out_proj, CORE)
        w_gate_other, w_up_other, w_down_other = (swap(w, CORE) for w in (w_gate, w_up, w_down))

        latent_out = attend(queries, cache, lengths)
        by_heads = lax.all_to_all(
            latent_out, "ep", split_axis=1, concat_axis=0, tiled=True,
            axis_index_groups=[list(range(c, devices, 2)) for c in (0, 1)],
        )

        orders = [relative_order(first, second, planes) for first, second in axes]
        experts = expert_slot.shape[0]
        labels = jnp.arange(experts, dtype=jnp.int32)
        physical = jnp.sum(
            jnp.where(routes[:, :, None] == labels, expert_slot[None, None, :], 0), axis=2
        )
        weights = jnp.sum(
            jnp.where(physical[:, :, None] == labels, gates[:, :, None], 0.0), axis=1
        )
        pieces = []
        for _ in range(3):
            piece = lax.reduce_precision(weights, 8, 7)
            pieces.append(piece.astype(BF16))
            weights = weights - piece
        tail = jnp.pad(jnp.concatenate(pieces, axis=1), ((0, 0), (0, 128 - 3 * experts)))

        even = core == 0
        heads_up = jnp.concatenate(
            [
                jnp.where(even, value_up, value_up_other),
                jnp.where(even, value_up_other, value_up),
            ],
            axis=0,
        )
        head_values = jnp.einsum(
            "bhl,hlv->bhv", by_heads, heads_up, preferred_element_type=F32
        ).astype(BF16)
        total_rows = head_values.shape[0]
        flat_values = head_values.reshape(total_rows, 2, -1)
        flat_values = jnp.concatenate(
            [
                jnp.where(even, flat_values[:, 0], flat_values[:, 1]),
                jnp.where(even, flat_values[:, 1], flat_values[:, 0]),
            ],
            axis=1,
        )
        picks = []
        for order in orders:
            place = jnp.bitwise_xor(jnp.asarray(order), me) // 2
            wanted = (place[:, None] * rows + jnp.arange(rows, dtype=jnp.int32)).reshape(-1, 1)
            pick = (wanted == jnp.arange(total_rows, dtype=jnp.int32)[None, :]).astype(BF16)
            picks.append(jnp.dot(pick, flat_values, preferred_element_type=F32).astype(BF16))
        cut = total_rows // 2
        own_rows = out_proj.shape[0]

        def out_part(g, part):
            x = picks[g][part * cut : (part + 1) * cut]
            span = slice(g * half, (g + 1) * half)
            return jnp.dot(
                x[:, :own_rows], out_proj[:, span], preferred_element_type=F32
            ) + jnp.dot(x[:, own_rows:], out_proj_other[:, span], preferred_element_type=F32)

        mixed = hidden.astype(F32) + sum_to_owner(out_part, rows)
        scale_rows = lax.rsqrt(jnp.mean(mixed * mixed, axis=1, keepdims=True) + norm_eps)
        normed = (mixed * scale_rows * norm_gain.astype(F32)).astype(BF16)

        tokens = to_all(jnp.concatenate([normed, tail], axis=1), half)
        tails = jnp.concatenate([t[:, half : half + 3 * experts] for t in tokens[1]], axis=0)
        w_in = jnp.concatenate([w_gate, w_gate_other, w_up, w_up_other], axis=1)
        w_out = jnp.concatenate([w_down, w_down_other], axis=0)

        def turn(x):
            return x.reshape(2, 2, planes * rows, -1).swapaxes(0, 1).reshape(total_rows, -1)

        acts = [
            jnp.concatenate(
                [
                    jnp.dot(
                        t[:, :half], w_in[g * half : (g + 1) * half], preferred_element_type=F32
                    )
                    for t in tokens[g]
                ],
                axis=0,
            )
            for g in (0, 1)
        ]
        acts = acts[0] + turn(acts[1])
        hid = acts.shape[1] // 2
        inner = (jax.nn.silu(acts[:, :hid]) * acts[:, hid:]).astype(BF16)
        inners = [inner, turn(inner)]
        mine = lax.broadcasted_iota(jnp.int32, tails.shape, 1) % experts == me // SLABS
        weight_b = jnp.sum(jnp.where(mine, tails.astype(F32), 0.0), axis=1, keepdims=True)
        weight_rows = [turn(weight_b), weight_b]

        def down_part(g, part):
            span = slice(part * cut, (part + 1) * cut)
            return weight_rows[g][span] * jnp.dot(
                inners[g][span], w_out[:, g * half : (g + 1) * half], preferred_element_type=F32
            )

        return (mixed + sum_to_owner(down_part, rows)).astype(BF16)

    return body


def solution(mesh):
    placed = (
        P(("groups", "ep"), None),
        P(("groups", "ep"), None, None),
        P(("groups", "ep"), None, None),
        P(("groups", "ep")),
        P("ep", None, None),
        P("ep", None),
        P(),
        P(("groups", "ep"), None),
        P(("groups", "ep"), None),
        P(),
        P(None, "ep"),
        P(None, "ep"),
        P("ep", None),
    )
    return jax.shard_map(
        on_device(mesh.shape["ep"]),
        mesh=mesh,
        in_specs=placed,
        out_specs=P(("groups", "ep"), None),
        check_vma=False,
    )
```

```python
import functools

import jax
import jax.numpy as jnp
import numpy as np
from jax import lax
from jax.experimental import pallas as pl
from jax.experimental.pallas import tpu as pltpu
from jax.sharding import PartitionSpec as P

LATENT = 512
SLABS = 8
F32 = jnp.float32
BF16 = jnp.bfloat16

score_scale = 192.0 ** (-0.5)
norm_eps = 1e-06

CORE, AX, AY = 1, 2, 4


def attend(queries, cache, lengths):
    scores = jnp.einsum("bhr,bpr->bhp", queries, cache, preferred_element_type=F32) * score_scale
    live_mask = lax.broadcasted_iota(jnp.int32, scores.shape, 2) < lengths[:, None, None]
    row_max = jnp.max(jnp.where(live_mask, scores, -jnp.inf), axis=2, keepdims=True)
    raised = jnp.where(live_mask, jnp.exp(scores - row_max), 0.0)
    probs_bf = (raised / jnp.sum(raised, axis=2, keepdims=True)).astype(BF16)
    return jnp.einsum(
        "bhp,bpl->bhl", probs_bf, cache[:, :, :LATENT], preferred_element_type=F32
    ).astype(BF16)


CHUNK = 512
LANES = 128
VMEM_BYTES = 12 * 1024 * 1024


def in_vmem(count):
    return [pl.BlockSpec(memory_space=pltpu.VMEM)] * count


def stage(arrays, shapes, copies_of, after):
    def body(*refs):
        ins, outs, sems = refs[: len(arrays)], refs[len(arrays) + 1 : -2], refs[-1]
        copies = [
            pltpu.make_async_copy(src, dst, sems.at[i])
            for i, (src, dst) in enumerate(copies_of(ins, outs))
        ]
        for copy in copies:
            copy.start()
        for copy in copies:
            copy.wait()
        refs[-2][...] = jnp.zeros_like(refs[-2])

    arrays = [pltpu.with_memory_space_constraint(w, pltpu.HBM) for w in arrays]
    count = 2 * len(arrays)
    size = sum(2 * int(np.prod(shape)) for shape in shapes)
    return pl.pallas_call(
        body,
        out_shape=tuple(pltpu.VMEM(shape, BF16) for shape in shapes)
        + (jax.ShapeDtypeStruct((8, 128), F32),),
        in_specs=[pl.BlockSpec(memory_space=pltpu.HBM)] * (len(arrays) + 1),
        out_specs=tuple(in_vmem(len(shapes) + 1)),
        scratch_shapes=[pltpu.SemaphoreType.DMA((count,))],
        compiler_params=pltpu.CompilerParams(vmem_limit_bytes=VMEM_BYTES),
        cost_estimate=pl.CostEstimate(flops=0, bytes_accessed=2 * size, transcendentals=0),
    )(*arrays, after)


def stage_columns(own, other, groups, after):
    depth, width = own.shape[0], own.shape[1] // groups

    def copies_of(ins, outs):
        return [
            (ref.at[:, pl.ds(g * width, width)], out.at[pl.ds(i * depth, depth)])
            for g, out in enumerate(outs)
            for i, ref in enumerate(ins)
        ]

    return stage((own, other), [(2 * depth, width)] * groups, copies_of, after)


def stage_beside(weights, after):
    depth, wide = weights[0].shape

    def copies_of(ins, outs):
        return [(ref, outs[0].at[:, pl.ds(i * wide, wide)]) for i, ref in enumerate(ins)]

    return stage(weights, [(depth, wide * len(weights))], copies_of, after)


def project_chunks(x, scale, w, send, keep):
    cut, width = keep.shape
    for c in range(width // CHUNK):
        span = pl.ds(c * CHUNK, CHUNK)
        y = jnp.dot(x, w[:, span], preferred_element_type=F32) * scale
        keep[:, span] = y[:cut]
        send[:, span] = y[cut:].astype(BF16)


def project_body(x, scale, w, send, keep):
    project_chunks(x[...], scale[...], w, send, keep)


def projected(rows, width):
    return (
        jax.ShapeDtypeStruct((rows // 2, width), BF16),
        jax.ShapeDtypeStruct((rows // 2, width), F32),
    )


def project(x, scale, w):
    rows, depth = x.shape
    width = w.shape[1]
    w = pltpu.with_memory_space_constraint(w, pltpu.VMEM)
    return pl.pallas_call(
        project_body,
        out_shape=projected(rows, width),
        in_specs=in_vmem(3),
        out_specs=tuple(in_vmem(2)),
        compiler_params=pltpu.CompilerParams(vmem_limit_bytes=VMEM_BYTES),
        cost_estimate=pl.CostEstimate(
            flops=2 * rows * depth * width, bytes_accessed=depth * width, transcendentals=0
        ),
    )(x, scale, w)


def stream_body(first, x, own, other, send, keep, held, total, sems):
    cut, width = keep.shape
    step = min(own.shape[0], 2 * LANES)
    per = own.shape[0] // step
    copies = [
        pltpu.make_async_copy(
            w.at[pl.ds(r * step, step), pl.ds(first, width)],
            held.at[pl.ds((i * per + r) * step, step)],
            sems.at[i, r],
        )
        for i, w in enumerate((own, other))
        for r in range(per)
    ]
    for copy in copies:
        copy.start()
    for k, copy in enumerate(copies):
        copy.wait()
        rows = x[:, k * step : (k + 1) * step]
        for c in range(width // CHUNK):
            span = pl.ds(c * CHUNK, CHUNK)
            y = jnp.dot(rows, held[pl.ds(k * step, step), span], preferred_element_type=F32)
            if k > 0:
                y = y + total[:, span]
            if k + 1 < len(copies):
                total[:, span] = y
            else:
                keep[:, span] = y[:cut]
                send[:, span] = y[cut:].astype(BF16)


def project_stream(x, own, other, first, width):
    rows, depth = x.shape
    own, other = (pltpu.with_memory_space_constraint(w, pltpu.HBM) for w in (own, other))
    return pl.pallas_call(
        functools.partial(stream_body, first),
        out_shape=projected(rows, width),
        in_specs=in_vmem(1) + [pl.BlockSpec(memory_space=pltpu.HBM)] * 2,
        out_specs=tuple(in_vmem(2)),
        scratch_shapes=[
            pltpu.VMEM((depth, width), BF16),
            pltpu.VMEM((rows, width), F32),
            pltpu.SemaphoreType.DMA((2, max(1, own.shape[0] // (2 * LANES)))),
        ],
        compiler_params=pltpu.CompilerParams(vmem_limit_bytes=2 * VMEM_BYTES),
        cost_estimate=pl.CostEstimate(
            flops=2 * rows * depth * width, bytes_accessed=2 * depth * width, transcendentals=0
        ),
    )(x, own, other)


def expert_body(
    block, label, near_a, far_a, near_b, far_b, w_in, w_out, send, keep, inner_b, weight_b
):
    cut, half = near_a.shape
    sums = []
    for g, (near, far) in enumerate(((near_a, far_a), (near_b, far_b))):
        total = jnp.zeros((2 * cut, w_in.shape[1]), F32)
        for c in range(half // CHUNK):
            span = pl.ds(c * CHUNK, CHUNK)
            x = jnp.concatenate([near[:, span], far[:, span]], axis=0)
            w = w_in[pl.ds(g * half + c * CHUNK, CHUNK)]
            total = total + jnp.dot(x, w, preferred_element_type=F32)
        sums.append(total)

    def turn(x):
        q = block
        return jnp.concatenate([x[:q], x[2 * q : 3 * q], x[q : 2 * q], x[3 * q :]], axis=0)

    acts = sums[0] + turn(sums[1])
    hid = acts.shape[1] // 2
    gates, ups = acts[:, :hid], acts[:, hid:]
    inner = gates / (1.0 + jnp.exp(-gates)) * ups
    tails = jnp.concatenate([near_b[:, half:], far_b[:, half:]], axis=0).astype(F32)
    lane = lax.broadcasted_iota(jnp.int32, tails.shape, 1)
    mine = lax.rem(lane, label[1]) == label[0]
    weight = jnp.sum(jnp.where(mine, tails, 0.0), axis=1, keepdims=True)
    weight_b[...] = weight
    inner_b[...] = turn(inner).astype(BF16)
    project_chunks(inner.astype(BF16), turn(weight), w_out, send, keep)


def expert(label, tokens, w_in, w_out):
    (near_a, far_a), (near_b, far_b) = tokens
    rows, half = 2 * near_a.shape[0], near_a.shape[1]
    hid = w_out.shape[0]
    w_in, w_out = (pltpu.with_memory_space_constraint(w, pltpu.VMEM) for w in (w_in, w_out))
    return pl.pallas_call(
        functools.partial(expert_body, rows // 4),
        out_shape=projected(rows, half)
        + (jax.ShapeDtypeStruct((rows, hid), BF16), jax.ShapeDtypeStruct((rows, 1), F32)),
        in_specs=[pl.BlockSpec(memory_space=pltpu.SMEM)] + in_vmem(6),
        out_specs=tuple(in_vmem(4)),
        compiler_params=pltpu.CompilerParams(vmem_limit_bytes=VMEM_BYTES),
        cost_estimate=pl.CostEstimate(
            flops=2 * rows * (w_in.size + w_out.size),
            bytes_accessed=w_in.size + w_out.size,
            transcendentals=rows * hid,
        ),
    )(label, near_a, far_a, near_b, far_b, w_in, w_out)


def relative_order(first, second, planes):
    return np.array(
        [
            z * SLABS + b * second + a * first
            for a in (0, 1)
            for b in (0, 1)
            for z in range(planes)
        ],
        np.int32,
    )


def on_device(devices):
    planes = devices // SLABS
    chips = devices // 2
    axes = ((AX, AY), (AY, AX))

    def swap(x, mask):
        return lax.ppermute(x, "ep", [(i, i ^ mask) for i in range(devices)])

    def sum_to_owner(products, rows):
        outs = []
        for g, (send, keep) in enumerate(products):
            x = keep + swap(send, axes[g][0]).astype(F32)
            half = x.shape[0] // 2
            outs.append(x[:half] + swap(x[half:].astype(BF16), axes[g][1]).astype(F32))
        x = jnp.concatenate(outs, axis=1)
        total = x[:rows]
        for d in range(1, planes):
            total = total + swap(x[d * rows : (d + 1) * rows].astype(BF16), d * SLABS).astype(F32)
        return total

    def to_all(x, cut):
        x = jnp.concatenate([x] + [swap(x, d * SLABS) for d in range(1, planes)], axis=0)
        near = [
            jnp.concatenate([part, swap(part, axes[g][1])], axis=0)
            for g, part in enumerate((x[:, :cut], x[:, cut:]))
        ]
        return [(near[g], swap(near[g], axes[g][0])) for g in (0, 1)]

    def body(
        hidden, queries, cache, lengths, value_up, out_proj, norm_gain,
        routes, gates, expert_slot, w_gate, w_up, w_down,
    ):
        rows, width = hidden.shape
        half = width // 2
        me = lax.axis_index("ep")
        core = me % 2
        value_up_other = swap(value_up, CORE)
        out_proj_other = swap(out_proj, CORE)
        w_gate_other, w_up_other, w_down_other = (swap(w, CORE) for w in (w_gate, w_up, w_down))

        latent_out = attend(queries, cache, lengths)
        by_heads = lax.all_to_all(
            latent_out, "ep", split_axis=1, concat_axis=0, tiled=True,
            axis_index_groups=[list(range(c, devices, 2)) for c in (0, 1)],
        )

        after = latent_out[0, :16, :128]
        w_in, _ = stage_beside((w_gate, w_gate_other, w_up, w_up_other), after)
        *w_out, _ = stage_columns(w_down, w_down_other, 2, after)
        even = core == 0
        heads_up = jnp.concatenate(
            [
                jnp.where(even, value_up, value_up_other),
                jnp.where(even, value_up_other, value_up),
            ],
            axis=0,
        )
        by_heads, heads_up = lax.optimization_barrier((by_heads, heads_up))

        orders = [relative_order(first, second, planes) for first, second in axes]
        experts = expert_slot.shape[0]
        labels = jnp.arange(experts, dtype=jnp.int32)
        physical = jnp.sum(
            jnp.where(routes[:, :, None] == labels, expert_slot[None, None, :], 0), axis=2
        )
        weights = jnp.sum(
            jnp.where(physical[:, :, None] == labels, gates[:, :, None], 0.0), axis=1
        )
        pieces = []
        for _ in range(3):
            piece = lax.reduce_precision(weights, 8, 7)
            pieces.append(piece.astype(BF16))
            weights = weights - piece
        tail = jnp.pad(jnp.concatenate(pieces, axis=1), ((0, 0), (0, 128 - 3 * experts)))

        head_values = jnp.einsum(
            "bhl,hlv->bhv", by_heads, heads_up, preferred_element_type=F32
        ).astype(BF16)
        total_rows = head_values.shape[0]
        flat_values = head_values.reshape(total_rows, 2, -1)
        flat_values = jnp.concatenate(
            [
                jnp.where(even, flat_values[:, 0], flat_values[:, 1]),
                jnp.where(even, flat_values[:, 1], flat_values[:, 0]),
            ],
            axis=1,
        )
        picks = []
        for order in orders:
            place = jnp.bitwise_xor(jnp.asarray(order), me) // 2
            wanted = (place[:, None] * rows + jnp.arange(rows, dtype=jnp.int32)).reshape(-1, 1)
            pick = (wanted == jnp.arange(total_rows, dtype=jnp.int32)[None, :]).astype(BF16)
            picks.append(jnp.dot(pick, flat_values, preferred_element_type=F32).astype(BF16))
        attended = sum_to_owner(
            [project_stream(picks[g], out_proj, out_proj_other, g * half, half) for g in (0, 1)],
            rows,
        )
        mixed = hidden.astype(F32) + attended
        scale_rows = lax.rsqrt(jnp.mean(mixed * mixed, axis=1, keepdims=True) + norm_eps)
        normed = (mixed * scale_rows * norm_gain.astype(F32)).astype(BF16)

        tokens = to_all(jnp.concatenate([normed, tail], axis=1), half)
        label = jnp.stack([me // SLABS, jnp.int32(experts)])
        *product_a, inner_b, weight_b = expert(label, tokens, w_in, w_out[0])
        product_b = project(inner_b, weight_b, w_out[1])
        return (mixed + sum_to_owner([product_a, product_b], rows)).astype(BF16)

    return body


def solution(mesh):
    placed = (
        P(("groups", "ep"), None),
        P(("groups", "ep"), None, None),
        P(("groups", "ep"), None, None),
        P(("groups", "ep")),
        P("ep", None, None),
        P("ep", None),
        P(),
        P(("groups", "ep"), None),
        P(("groups", "ep"), None),
        P(),
        P(None, "ep"),
        P(None, "ep"),
        P("ep", None),
    )
    return jax.shard_map(
        on_device(mesh.shape["ep"]),
        mesh=mesh,
        in_specs=placed,
        out_specs=P(("groups", "ep"), None),
        check_vma=False,
    )
```

```python
import functools

import jax
import jax.numpy as jnp
import numpy as np
from jax import lax
from jax.experimental import pallas as pl
from jax.experimental.pallas import tpu as pltpu
from jax.sharding import PartitionSpec as P

LATENT = 512
SLABS = 8
F32 = jnp.float32
BF16 = jnp.bfloat16

score_scale = 192.0 ** (-0.5)
norm_eps = 1e-06

CORE, AX, AY = 1, 2, 4


def attend(queries, cache, lengths):
    scores = jnp.einsum("bhr,bpr->bhp", queries, cache, preferred_element_type=F32) * score_scale
    live_mask = lax.broadcasted_iota(jnp.int32, scores.shape, 2) < lengths[:, None, None]
    row_max = jnp.max(jnp.where(live_mask, scores, -jnp.inf), axis=2, keepdims=True)
    raised = jnp.where(live_mask, jnp.exp(scores - row_max), 0.0)
    probs_bf = (raised / jnp.sum(raised, axis=2, keepdims=True)).astype(BF16)
    return jnp.einsum(
        "bhp,bpl->bhl", probs_bf, cache[:, :, :LATENT], preferred_element_type=F32
    ).astype(BF16)


CHUNK = 512
LANES = 128
VMEM_BYTES = 12 * 1024 * 1024


def in_vmem(count):
    return [pl.BlockSpec(memory_space=pltpu.VMEM)] * count


def stage(arrays, shapes, copies_of, after):
    def body(*refs):
        ins, outs, sems = refs[: len(arrays)], refs[len(arrays) + 1 : -2], refs[-1]
        copies = [
            pltpu.make_async_copy(src, dst, sems.at[i])
            for i, (src, dst) in enumerate(copies_of(ins, outs))
        ]
        for copy in copies:
            copy.start()
        for copy in copies:
            copy.wait()
        refs[-2][...] = jnp.zeros_like(refs[-2])

    arrays = [pltpu.with_memory_space_constraint(w, pltpu.HBM) for w in arrays]
    count = 2 * len(arrays)
    size = sum(2 * int(np.prod(shape)) for shape in shapes)
    return pl.pallas_call(
        body,
        out_shape=tuple(pltpu.VMEM(shape, BF16) for shape in shapes)
        + (jax.ShapeDtypeStruct((8, 128), F32),),
        in_specs=[pl.BlockSpec(memory_space=pltpu.HBM)] * len(arrays)
        + [pl.BlockSpec(memory_space=pl.ANY)],
        out_specs=tuple(in_vmem(len(shapes) + 1)),
        scratch_shapes=[pltpu.SemaphoreType.DMA((count,))],
        compiler_params=pltpu.CompilerParams(vmem_limit_bytes=VMEM_BYTES),
        cost_estimate=pl.CostEstimate(flops=0, bytes_accessed=2 * size, transcendentals=0),
    )(*arrays, after)


def stage_columns(own, other, groups, after):
    depth, width = own.shape[0], own.shape[1] // groups

    def copies_of(ins, outs):
        return [
            (ref.at[:, pl.ds(g * width, width)], out.at[pl.ds(i * depth, depth)])
            for g, out in enumerate(outs)
            for i, ref in enumerate(ins)
        ]

    return stage((own, other), [(2 * depth, width)] * groups, copies_of, after)


def stage_beside(weights, after):
    depth, wide = weights[0].shape

    def copies_of(ins, outs):
        return [(ref, outs[0].at[:, pl.ds(i * wide, wide)]) for i, ref in enumerate(ins)]

    return stage(weights, [(depth, wide * len(weights))], copies_of, after)


def projected(rows, width):
    return (
        jax.ShapeDtypeStruct((rows // 2, width), BF16),
        jax.ShapeDtypeStruct((rows // 2, width), F32),
    )


def stream_body(picked, own, other, *refs):
    *outs, held, total, sems = refs
    groups = len(outs) // 2
    cut, width = outs[0].shape
    step = min(own.shape[0], 2 * LANES)
    per = own.shape[0] // step
    copies = [
        pltpu.make_async_copy(
            w.at[pl.ds(r * step, step)], held.at[pl.ds((i * per + r) * step, step)], sems.at[i, r]
        )
        for i, w in enumerate((own, other))
        for r in range(per)
    ]
    for copy in copies:
        copy.start()
    for k, copy in enumerate(copies):
        copy.wait()
        for g in range(groups):
            send, keep = outs[2 * g : 2 * g + 2]
            rows = picked[g, :, k * step : (k + 1) * step]
            for c in range(width // CHUNK):
                span = pl.ds(c * CHUNK, CHUNK)
                wide = pl.ds(g * width + c * CHUNK, CHUNK)
                y = jnp.dot(rows, held[pl.ds(k * step, step), wide], preferred_element_type=F32)
                if k > 0:
                    y = y + total[:, wide]
                if k + 1 < len(copies):
                    total[:, wide] = y
                else:
                    keep[:, span] = y[:cut]
                    send[:, span] = y[cut:].astype(BF16)


def project_stream(picked, own, other):
    groups, rows, depth = picked.shape
    width = own.shape[1]
    own, other = (pltpu.with_memory_space_constraint(w, pltpu.HBM) for w in (own, other))
    outs = pl.pallas_call(
        stream_body,
        out_shape=projected(rows, width // groups) * groups,
        in_specs=in_vmem(1) + [pl.BlockSpec(memory_space=pltpu.HBM)] * 2,
        out_specs=tuple(in_vmem(2 * groups)),
        scratch_shapes=[
            pltpu.VMEM((depth, width), BF16),
            pltpu.VMEM((rows, width), F32),
            pltpu.SemaphoreType.DMA((2, max(1, own.shape[0] // (2 * LANES)))),
        ],
        compiler_params=pltpu.CompilerParams(vmem_limit_bytes=3 * VMEM_BYTES),
        cost_estimate=pl.CostEstimate(
            flops=2 * rows * depth * width, bytes_accessed=2 * depth * width, transcendentals=0
        ),
    )(picked, own, other)
    return [outs[2 * g : 2 * g + 2] for g in range(groups)]


def expert_body(
    block, label, near_a, far_a, near_b, far_b, w_in, w_out_a, w_out_b, *outs
):
    cut, half = near_a.shape
    sums = []
    for g, (near, far) in enumerate(((near_a, far_a), (near_b, far_b))):
        total = jnp.zeros((2 * cut, w_in.shape[1]), F32)
        for c in range(half // CHUNK):
            span = pl.ds(c * CHUNK, CHUNK)
            x = jnp.concatenate([near[:, span], far[:, span]], axis=0)
            w = w_in[pl.ds(g * half + c * CHUNK, CHUNK)]
            total = total + jnp.dot(x, w, preferred_element_type=F32)
        sums.append(total)

    def turn(x):
        q = block
        return jnp.concatenate([x[:q], x[2 * q : 3 * q], x[q : 2 * q], x[3 * q :]], axis=0)

    acts = sums[0] + turn(sums[1])
    hid = acts.shape[1] // 2
    gates, ups = acts[:, :hid], acts[:, hid:]
    inner = gates / (1.0 + jnp.exp(-gates)) * ups
    tails = jnp.concatenate([near_b[:, half:], far_b[:, half:]], axis=0).astype(F32)
    lane = lax.broadcasted_iota(jnp.int32, tails.shape, 1)
    mine = lax.rem(lane, label[1]) == label[0]
    weight = jnp.sum(jnp.where(mine, tails, 0.0), axis=1, keepdims=True)
    for g, w_out in enumerate((w_out_a, w_out_b)):
        send, keep = outs[2 * g : 2 * g + 2]
        x = (inner if g == 0 else turn(inner)).astype(BF16)
        scale = turn(weight) if g == 0 else weight
        for c in range(half // CHUNK):
            span = pl.ds(c * CHUNK, CHUNK)
            y = jnp.dot(x, w_out[:, span], preferred_element_type=F32) * scale
            keep[:, span] = y[:cut]
            send[:, span] = y[cut:].astype(BF16)


def expert(label, tokens, w_in, w_out):
    (near_a, far_a), (near_b, far_b) = tokens
    rows, half = 2 * near_a.shape[0], near_a.shape[1]
    hid = w_out[0].shape[0]
    w_in, *w_out = (pltpu.with_memory_space_constraint(w, pltpu.VMEM) for w in (w_in, *w_out))
    outs = pl.pallas_call(
        functools.partial(expert_body, rows // 4),
        out_shape=projected(rows, half) * 2,
        in_specs=[pl.BlockSpec(memory_space=pltpu.SMEM)] + in_vmem(7),
        out_specs=tuple(in_vmem(4)),
        compiler_params=pltpu.CompilerParams(vmem_limit_bytes=VMEM_BYTES),
        cost_estimate=pl.CostEstimate(
            flops=2 * rows * (w_in.size + 2 * w_out[0].size),
            bytes_accessed=w_in.size + 2 * w_out[0].size,
            transcendentals=rows * hid,
        ),
    )(label, near_a, far_a, near_b, far_b, w_in, *w_out)
    return outs[:2], outs[2:]


def relative_order(first, second, planes):
    return np.array(
        [
            z * SLABS + b * second + a * first
            for a in (0, 1)
            for b in (0, 1)
            for z in range(planes)
        ],
        np.int32,
    )


def on_device(devices):
    planes = devices // SLABS
    chips = devices // 2
    axes = ((AX, AY), (AY, AX))

    def swap(x, mask):
        return lax.ppermute(x, "ep", [(i, i ^ mask) for i in range(devices)])

    def sum_to_owner(products, rows):
        outs = []
        for g, (send, keep) in enumerate(products):
            x = keep + swap(send, axes[g][0]).astype(F32)
            half = x.shape[0] // 2
            outs.append(x[:half] + swap(x[half:].astype(BF16), axes[g][1]).astype(F32))
        x = jnp.concatenate(outs, axis=1)
        total = x[:rows]
        for d in range(1, planes):
            total = total + swap(x[d * rows : (d + 1) * rows].astype(BF16), d * SLABS).astype(F32)
        return total

    def to_all(x, cut):
        x = jnp.concatenate([x] + [swap(x, d * SLABS) for d in range(1, planes)], axis=0)
        near = [
            jnp.concatenate([part, swap(part, axes[g][1])], axis=0)
            for g, part in enumerate((x[:, :cut], x[:, cut:]))
        ]
        return [(near[g], swap(near[g], axes[g][0])) for g in (0, 1)]

    def body(
        hidden, queries, cache, lengths, value_up, out_proj, norm_gain,
        routes, gates, expert_slot, w_gate, w_up, w_down,
    ):
        rows, width = hidden.shape
        half = width // 2
        me = lax.axis_index("ep")
        core = me % 2
        value_up_other = swap(value_up, CORE)
        out_proj_other = swap(out_proj, CORE)
        w_gate_other, w_up_other, w_down_other = (swap(w, CORE) for w in (w_gate, w_up, w_down))

        latent_out = attend(queries, cache, lengths)
        by_heads = lax.all_to_all(
            latent_out, "ep", split_axis=1, concat_axis=0, tiled=True,
            axis_index_groups=[list(range(c, devices, 2)) for c in (0, 1)],
        )

        even = core == 0
        heads_up = jnp.concatenate(
            [
                jnp.where(even, value_up, value_up_other),
                jnp.where(even, value_up_other, value_up),
            ],
            axis=0,
        )
        by_heads, heads_up, w_gate_other, w_up_other, w_down_other = lax.optimization_barrier(
            (by_heads, heads_up, w_gate_other, w_up_other, w_down_other)
        )

        orders = [relative_order(first, second, planes) for first, second in axes]
        experts = expert_slot.shape[0]
        labels = jnp.arange(experts, dtype=jnp.int32)
        physical = jnp.sum(
            jnp.where(routes[:, :, None] == labels, expert_slot[None, None, :], 0), axis=2
        )
        weights = jnp.sum(
            jnp.where(physical[:, :, None] == labels, gates[:, :, None], 0.0), axis=1
        )
        pieces = []
        for _ in range(3):
            piece = lax.reduce_precision(weights, 8, 7)
            pieces.append(piece.astype(BF16))
            weights = weights - piece
        tail = jnp.pad(jnp.concatenate(pieces, axis=1), ((0, 0), (0, 128 - 3 * experts)))

        head_values = jnp.einsum(
            "bhl,hlv->bhv", by_heads, heads_up, preferred_element_type=F32
        ).astype(BF16)
        total_rows = head_values.shape[0]
        flat_values = head_values.reshape(total_rows, 2, -1)
        flat_values = jnp.concatenate(
            [
                jnp.where(even, flat_values[:, 0], flat_values[:, 1]),
                jnp.where(even, flat_values[:, 1], flat_values[:, 0]),
            ],
            axis=1,
        )
        picks = []
        for order in orders:
            place = jnp.bitwise_xor(jnp.asarray(order), me) // 2
            wanted = (place[:, None] * rows + jnp.arange(rows, dtype=jnp.int32)).reshape(-1, 1)
            picks.append(wanted == jnp.arange(total_rows, dtype=jnp.int32)[None, :])
        picks = jnp.concatenate(picks, axis=0).astype(BF16)
        picked = jnp.dot(picks, flat_values, preferred_element_type=F32).astype(BF16)
        products = project_stream(picked.reshape(2, total_rows, -1), out_proj, out_proj_other)
        attended = sum_to_owner(products, rows)
        mixed = hidden.astype(F32) + attended
        scale_rows = lax.rsqrt(jnp.mean(mixed * mixed, axis=1, keepdims=True) + norm_eps)
        normed = (mixed * scale_rows * norm_gain.astype(F32)).astype(BF16)

        w_in, _ = stage_beside((w_gate, w_gate_other, w_up, w_up_other), normed)
        *w_out, _ = stage_columns(w_down, w_down_other, 2, normed)
        tokens = to_all(jnp.concatenate([normed, tail], axis=1), half)
        label = jnp.stack([me // SLABS, jnp.int32(experts)])
        products = expert(label, tokens, w_in, w_out)
        return (mixed + sum_to_owner(products, rows)).astype(BF16)

    return body


def solution(mesh):
    placed = (
        P(("groups", "ep"), None),
        P(("groups", "ep"), None, None),
        P(("groups", "ep"), None, None),
        P(("groups", "ep")),
        P("ep", None, None),
        P("ep", None),
        P(),
        P(("groups", "ep"), None),
        P(("groups", "ep"), None),
        P(),
        P(None, "ep"),
        P(None, "ep"),
        P("ep", None),
    )
    return jax.shard_map(
        on_device(mesh.shape["ep"]),
        mesh=mesh,
        in_specs=placed,
        out_specs=P(("groups", "ep"), None),
        check_vma=False,
    )
```

```python
import functools

import jax
import jax.numpy as jnp
import numpy as np
from jax import lax
from jax.experimental import pallas as pl
from jax.experimental.pallas import tpu as pltpu
from jax.sharding import PartitionSpec as P

LATENT = 512
SLABS = 8
F32 = jnp.float32
BF16 = jnp.bfloat16

score_scale = 192.0 ** (-0.5)
norm_eps = 1e-06

CORE, AX, AY = 1, 2, 4


def attend(queries, cache, lengths):
    scores = jnp.einsum("bhr,bpr->bhp", queries, cache, preferred_element_type=F32) * score_scale
    live_mask = lax.broadcasted_iota(jnp.int32, scores.shape, 2) < lengths[:, None, None]
    row_max = jnp.max(jnp.where(live_mask, scores, -jnp.inf), axis=2, keepdims=True)
    raised = jnp.where(live_mask, jnp.exp(scores - row_max), 0.0)
    probs_bf = (raised / jnp.sum(raised, axis=2, keepdims=True)).astype(BF16)
    return jnp.einsum(
        "bhp,bpl->bhl", probs_bf, cache[:, :, :LATENT], preferred_element_type=F32
    ).astype(BF16)


CHUNK = 512
LANES = 128
VMEM_BYTES = 12 * 1024 * 1024


def in_vmem(count):
    return [pl.BlockSpec(memory_space=pltpu.VMEM)] * count


def stage(arrays, shapes, copies_of, after):
    def body(*refs):
        ins, outs, sems = refs[: len(arrays)], refs[len(arrays) + 1 : -2], refs[-1]
        copies = [
            pltpu.make_async_copy(src, dst, sems.at[i])
            for i, (src, dst) in enumerate(copies_of(ins, outs))
        ]
        for copy in copies:
            copy.start()
        for copy in copies:
            copy.wait()
        refs[-2][...] = jnp.zeros_like(refs[-2])

    arrays = [pltpu.with_memory_space_constraint(w, pltpu.HBM) for w in arrays]
    count = 2 * len(arrays)
    size = sum(2 * int(np.prod(shape)) for shape in shapes)
    return pl.pallas_call(
        body,
        out_shape=tuple(pltpu.VMEM(shape, BF16) for shape in shapes)
        + (jax.ShapeDtypeStruct((8, 128), F32),),
        in_specs=[pl.BlockSpec(memory_space=pltpu.HBM)] * len(arrays)
        + [pl.BlockSpec(memory_space=pl.ANY)],
        out_specs=tuple(in_vmem(len(shapes) + 1)),
        scratch_shapes=[pltpu.SemaphoreType.DMA((count,))],
        compiler_params=pltpu.CompilerParams(vmem_limit_bytes=VMEM_BYTES),
        cost_estimate=pl.CostEstimate(flops=0, bytes_accessed=2 * size, transcendentals=0),
    )(*arrays, after)


def stage_columns(own, other, groups, after):
    depth, width = own.shape[0], own.shape[1] // groups

    def copies_of(ins, outs):
        return [
            (ref.at[:, pl.ds(g * width, width)], out.at[pl.ds(i * depth, depth)])
            for g, out in enumerate(outs)
            for i, ref in enumerate(ins)
        ]

    return stage((own, other), [(2 * depth, width)] * groups, copies_of, after)


def stage_beside(weights, after):
    depth, wide = weights[0].shape

    def copies_of(ins, outs):
        return [(ref, outs[0].at[:, pl.ds(i * wide, wide)]) for i, ref in enumerate(ins)]

    return stage(weights, [(depth, wide * len(weights))], copies_of, after)


def projected(rows, width):
    return (
        jax.ShapeDtypeStruct((rows // 2, width), BF16),
        jax.ShapeDtypeStruct((rows // 2, width), F32),
    )


def stream_body(picked, own, other, *refs):
    *outs, held, total, sems = refs
    groups = len(outs) // 2
    cut, width = outs[0].shape
    step = min(own.shape[0], 2 * LANES)
    per = own.shape[0] // step
    copies = [
        pltpu.make_async_copy(
            w.at[pl.ds(r * step, step)], held.at[pl.ds((i * per + r) * step, step)], sems.at[i, r]
        )
        for i, w in enumerate((own, other))
        for r in range(per)
    ]
    for copy in copies:
        copy.start()
    for k, copy in enumerate(copies):
        copy.wait()
        for g in range(groups):
            send, keep = outs[2 * g : 2 * g + 2]
            rows = picked[g, :, k * step : (k + 1) * step]
            for c in range(width // CHUNK):
                span = pl.ds(c * CHUNK, CHUNK)
                wide = pl.ds(g * width + c * CHUNK, CHUNK)
                y = jnp.dot(rows, held[pl.ds(k * step, step), wide], preferred_element_type=F32)
                if k > 0:
                    y = y + total[:, wide]
                if k + 1 < len(copies):
                    total[:, wide] = y
                else:
                    keep[:, span] = y[:cut]
                    send[:, span] = y[cut:].astype(BF16)


def project_stream(picked, own, other):
    groups, rows, depth = picked.shape
    width = own.shape[1]
    own, other = (pltpu.with_memory_space_constraint(w, pltpu.HBM) for w in (own, other))
    outs = pl.pallas_call(
        stream_body,
        out_shape=projected(rows, width // groups) * groups,
        in_specs=in_vmem(1) + [pl.BlockSpec(memory_space=pltpu.HBM)] * 2,
        out_specs=tuple(in_vmem(2 * groups)),
        scratch_shapes=[
            pltpu.VMEM((depth, width), BF16),
            pltpu.VMEM((rows, width), F32),
            pltpu.SemaphoreType.DMA((2, max(1, own.shape[0] // (2 * LANES)))),
        ],
        compiler_params=pltpu.CompilerParams(vmem_limit_bytes=3 * VMEM_BYTES),
        cost_estimate=pl.CostEstimate(
            flops=2 * rows * depth * width, bytes_accessed=2 * depth * width, transcendentals=0
        ),
    )(picked, own, other)
    return [outs[2 * g : 2 * g + 2] for g in range(groups)]


def expert_body(
    block, label, near_a, far_a, near_b, far_b, w_in, w_out_a, w_out_b, *outs
):
    cut, half = near_a.shape
    sums = []
    for g, (near, far) in enumerate(((near_a, far_a), (near_b, far_b))):
        total = jnp.zeros((2 * cut, w_in.shape[1]), F32)
        for c in range(half // CHUNK):
            span = pl.ds(c * CHUNK, CHUNK)
            x = jnp.concatenate([near[:, span], far[:, span]], axis=0)
            w = w_in[pl.ds(g * half + c * CHUNK, CHUNK)]
            total = total + jnp.dot(x, w, preferred_element_type=F32)
        sums.append(total)

    def turn(x):
        q = block
        return jnp.concatenate([x[:q], x[2 * q : 3 * q], x[q : 2 * q], x[3 * q :]], axis=0)

    acts = sums[0] + turn(sums[1])
    hid = acts.shape[1] // 2
    gates, ups = acts[:, :hid], acts[:, hid:]
    inner = gates / (1.0 + jnp.exp(-gates)) * ups
    tails = jnp.concatenate([near_b[:, half:], far_b[:, half:]], axis=0).astype(F32)
    lane = lax.broadcasted_iota(jnp.int32, tails.shape, 1)
    mine = lax.rem(lane, label[1]) == label[0]
    weight = jnp.sum(jnp.where(mine, tails, 0.0), axis=1, keepdims=True)
    for g, w_out in enumerate((w_out_a, w_out_b)):
        send, keep = outs[2 * g : 2 * g + 2]
        x = (inner if g == 0 else turn(inner)).astype(BF16)
        scale = turn(weight) if g == 0 else weight
        for c in range(half // CHUNK):
            span = pl.ds(c * CHUNK, CHUNK)
            y = jnp.dot(x, w_out[:, span], preferred_element_type=F32) * scale
            keep[:, span] = y[:cut]
            send[:, span] = y[cut:].astype(BF16)


def expert(label, tokens, w_in, w_out):
    (near_a, far_a), (near_b, far_b) = tokens
    rows, half = 2 * near_a.shape[0], near_a.shape[1]
    hid = w_out[0].shape[0]
    w_in, *w_out = (pltpu.with_memory_space_constraint(w, pltpu.VMEM) for w in (w_in, *w_out))
    outs = pl.pallas_call(
        functools.partial(expert_body, rows // 4),
        out_shape=projected(rows, half) * 2,
        in_specs=[pl.BlockSpec(memory_space=pltpu.SMEM)] + in_vmem(7),
        out_specs=tuple(in_vmem(4)),
        compiler_params=pltpu.CompilerParams(vmem_limit_bytes=VMEM_BYTES),
        cost_estimate=pl.CostEstimate(
            flops=2 * rows * (w_in.size + 2 * w_out[0].size),
            bytes_accessed=w_in.size + 2 * w_out[0].size,
            transcendentals=rows * hid,
        ),
    )(label, near_a, far_a, near_b, far_b, w_in, *w_out)
    return outs[:2], outs[2:]


def relative_order(first, second, planes):
    return np.array(
        [
            z * SLABS + b * second + a * first
            for a in (0, 1)
            for b in (0, 1)
            for z in range(planes)
        ],
        np.int32,
    )


def on_device(devices):
    planes = devices // SLABS
    chips = devices // 2
    axes = ((AX, AY), (AY, AX))

    def swap(x, mask):
        return lax.ppermute(x, "ep", [(i, i ^ mask) for i in range(devices)])

    def sum_to_owner(products, rows):
        outs = []
        for g, (send, keep) in enumerate(products):
            x = keep + swap(send, axes[g][0]).astype(F32)
            half = x.shape[0] // 2
            outs.append(x[:half] + swap(x[half:].astype(BF16), axes[g][1]).astype(F32))
        x = jnp.concatenate(outs, axis=1)
        total = x[:rows]
        for d in reversed(range(1, planes)):
            total = total + swap(x[d * rows : (d + 1) * rows].astype(BF16), d * SLABS).astype(F32)
        return total

    def to_all(x, cut):
        far = [swap(x, d * SLABS) for d in reversed(range(1, planes))]
        x = jnp.concatenate([x] + far[::-1], axis=0)
        near = [
            jnp.concatenate([part, swap(part, axes[g][1])], axis=0)
            for g, part in enumerate((x[:, :cut], x[:, cut:]))
        ]
        return [(near[g], swap(near[g], axes[g][0])) for g in (0, 1)]

    def body(
        hidden, queries, cache, lengths, value_up, out_proj, norm_gain,
        routes, gates, expert_slot, w_gate, w_up, w_down,
    ):
        rows, width = hidden.shape
        half = width // 2
        me = lax.axis_index("ep")
        core = me % 2
        value_up_other = swap(value_up, CORE)
        out_proj_other = swap(out_proj, CORE)
        w_gate_other, w_up_other, w_down_other = (swap(w, CORE) for w in (w_gate, w_up, w_down))

        latent_out = attend(queries, cache, lengths)
        by_heads = lax.all_to_all(
            latent_out, "ep", split_axis=1, concat_axis=0, tiled=True,
            axis_index_groups=[list(range(c, devices, 2)) for c in (0, 1)],
        )

        even = core == 0
        heads_up = jnp.concatenate(
            [
                jnp.where(even, value_up, value_up_other),
                jnp.where(even, value_up_other, value_up),
            ],
            axis=0,
        )
        by_heads, heads_up, w_gate_other, w_up_other, w_down_other = lax.optimization_barrier(
            (by_heads, heads_up, w_gate_other, w_up_other, w_down_other)
        )

        orders = [relative_order(first, second, planes) for first, second in axes]
        experts = expert_slot.shape[0]
        labels = jnp.arange(experts, dtype=jnp.int32)
        physical = jnp.sum(
            jnp.where(routes[:, :, None] == labels, expert_slot[None, None, :], 0), axis=2
        )
        weights = jnp.sum(
            jnp.where(physical[:, :, None] == labels, gates[:, :, None], 0.0), axis=1
        )
        pieces = []
        for _ in range(3):
            piece = lax.reduce_precision(weights, 8, 7)
            pieces.append(piece.astype(BF16))
            weights = weights - piece
        tail = jnp.pad(jnp.concatenate(pieces, axis=1), ((0, 0), (0, 128 - 3 * experts)))

        head_values = jnp.einsum(
            "bhl,hlv->bhv", by_heads, heads_up, preferred_element_type=F32
        ).astype(BF16)
        total_rows = head_values.shape[0]
        flat_values = head_values.reshape(total_rows, 2, -1)
        flat_values = jnp.concatenate(
            [
                jnp.where(even, flat_values[:, 0], flat_values[:, 1]),
                jnp.where(even, flat_values[:, 1], flat_values[:, 0]),
            ],
            axis=1,
        )
        picks = []
        for order in orders:
            place = jnp.bitwise_xor(jnp.asarray(order), me) // 2
            wanted = (place[:, None] * rows + jnp.arange(rows, dtype=jnp.int32)).reshape(-1, 1)
            picks.append(wanted == jnp.arange(total_rows, dtype=jnp.int32)[None, :])
        picks = jnp.concatenate(picks, axis=0).astype(BF16)
        picked = jnp.dot(picks, flat_values, preferred_element_type=F32).astype(BF16)
        products = project_stream(picked.reshape(2, total_rows, -1), out_proj, out_proj_other)
        attended = sum_to_owner(products, rows)
        mixed = hidden.astype(F32) + attended
        scale_rows = lax.rsqrt(jnp.mean(mixed * mixed, axis=1, keepdims=True) + norm_eps)
        normed = (mixed * scale_rows * norm_gain.astype(F32)).astype(BF16)

        w_in, _ = stage_beside((w_gate, w_gate_other, w_up, w_up_other), normed)
        *w_out, _ = stage_columns(w_down, w_down_other, 2, normed)
        tokens = to_all(jnp.concatenate([normed, tail], axis=1), half)
        label = jnp.stack([me // SLABS, jnp.int32(experts)])
        products = expert(label, tokens, w_in, w_out)
        return (mixed + sum_to_owner(products, rows)).astype(BF16)

    return body


def solution(mesh):
    placed = (
        P(("groups", "ep"), None),
        P(("groups", "ep"), None, None),
        P(("groups", "ep"), None, None),
        P(("groups", "ep")),
        P("ep", None, None),
        P("ep", None),
        P(),
        P(("groups", "ep"), None),
        P(("groups", "ep"), None),
        P(),
        P(None, "ep"),
        P(None, "ep"),
        P("ep", None),
    )
    return jax.shard_map(
        on_device(mesh.shape["ep"]),
        mesh=mesh,
        in_specs=placed,
        out_specs=P(("groups", "ep"), None),
        check_vma=False,
    )
```

```python
import functools

import jax
import jax.numpy as jnp
import numpy as np
from jax import lax
from jax.experimental import pallas as pl
from jax.experimental.pallas import tpu as pltpu
from jax.sharding import PartitionSpec as P

LATENT = 512
SLABS = 8
F32 = jnp.float32
BF16 = jnp.bfloat16

score_scale = 192.0 ** (-0.5)
norm_eps = 1e-06

CORE, AX, AY = 1, 2, 4


def attend(queries, cache, lengths):
    scores = jnp.einsum("bhr,bpr->bhp", queries, cache, preferred_element_type=F32) * score_scale
    live_mask = lax.broadcasted_iota(jnp.int32, scores.shape, 2) < lengths[:, None, None]
    row_max = jnp.max(jnp.where(live_mask, scores, -jnp.inf), axis=2, keepdims=True)
    raised = jnp.where(live_mask, jnp.exp(scores - row_max), 0.0)
    probs_bf = (raised / jnp.sum(raised, axis=2, keepdims=True)).astype(BF16)
    return jnp.einsum(
        "bhp,bpl->bhl", probs_bf, cache[:, :, :LATENT], preferred_element_type=F32
    ).astype(BF16)


CHUNK = 512
LANES = 128
VMEM_BYTES = 12 * 1024 * 1024


def in_vmem(count):
    return [pl.BlockSpec(memory_space=pltpu.VMEM)] * count


def stage(arrays, shapes, copies_of, after):
    def body(*refs):
        ins, outs, sems = refs[: len(arrays)], refs[len(arrays) + 1 : -2], refs[-1]
        copies = [
            pltpu.make_async_copy(src, dst, sems.at[i])
            for i, (src, dst) in enumerate(copies_of(ins, outs))
        ]
        for copy in copies:
            copy.start()
        for copy in copies:
            copy.wait()
        refs[-2][...] = jnp.zeros_like(refs[-2])

    arrays = [pltpu.with_memory_space_constraint(w, pltpu.HBM) for w in arrays]
    count = 2 * len(arrays)
    size = sum(2 * int(np.prod(shape)) for shape in shapes)
    return pl.pallas_call(
        body,
        out_shape=tuple(pltpu.VMEM(shape, BF16) for shape in shapes)
        + (jax.ShapeDtypeStruct((8, 128), F32),),
        in_specs=[pl.BlockSpec(memory_space=pltpu.HBM)] * len(arrays)
        + [pl.BlockSpec(memory_space=pl.ANY)],
        out_specs=tuple(in_vmem(len(shapes) + 1)),
        scratch_shapes=[pltpu.SemaphoreType.DMA((count,))],
        compiler_params=pltpu.CompilerParams(vmem_limit_bytes=VMEM_BYTES),
        cost_estimate=pl.CostEstimate(flops=0, bytes_accessed=2 * size, transcendentals=0),
    )(*arrays, after)


def stage_columns(own, other, groups, after):
    depth, width = own.shape[0], own.shape[1] // groups

    def copies_of(ins, outs):
        return [
            (ref.at[:, pl.ds(g * width, width)], out.at[pl.ds(i * depth, depth)])
            for g, out in enumerate(outs)
            for i, ref in enumerate(ins)
        ]

    return stage((own, other), [(2 * depth, width)] * groups, copies_of, after)


def stage_beside(weights, after):
    depth, wide = weights[0].shape

    def copies_of(ins, outs):
        return [(ref, outs[0].at[:, pl.ds(i * wide, wide)]) for i, ref in enumerate(ins)]

    return stage(weights, [(depth, wide * len(weights))], copies_of, after)


def projected(rows, width):
    return (
        jax.ShapeDtypeStruct((rows // 2, width), BF16),
        jax.ShapeDtypeStruct((rows // 2, width), F32),
    )


def stream_body(picked, own, other, *refs):
    *outs, held, total, sems = refs
    groups = len(outs) // 2
    cut, width = outs[0].shape
    step = min(own.shape[0], 2 * LANES)
    per = own.shape[0] // step
    copies = [
        pltpu.make_async_copy(
            w.at[pl.ds(r * step, step)], held.at[pl.ds((i * per + r) * step, step)], sems.at[i, r]
        )
        for i, w in enumerate((own, other))
        for r in range(per)
    ]
    for copy in copies:
        copy.start()
    for k, copy in enumerate(copies):
        copy.wait()
        for g in range(groups):
            send, keep = outs[2 * g : 2 * g + 2]
            rows = picked[g, :, k * step : (k + 1) * step]
            for c in range(width // CHUNK):
                span = pl.ds(c * CHUNK, CHUNK)
                wide = pl.ds(g * width + c * CHUNK, CHUNK)
                y = jnp.dot(rows, held[pl.ds(k * step, step), wide], preferred_element_type=F32)
                if k > 0:
                    y = y + total[:, wide]
                if k + 1 < len(copies):
                    total[:, wide] = y
                else:
                    keep[:, span] = y[:cut]
                    send[:, span] = y[cut:].astype(BF16)


def project_stream(picked, own, other):
    groups, rows, depth = picked.shape
    width = own.shape[1]
    own, other = (pltpu.with_memory_space_constraint(w, pltpu.HBM) for w in (own, other))
    outs = pl.pallas_call(
        stream_body,
        out_shape=projected(rows, width // groups) * groups,
        in_specs=in_vmem(1) + [pl.BlockSpec(memory_space=pltpu.HBM)] * 2,
        out_specs=tuple(in_vmem(2 * groups)),
        scratch_shapes=[
            pltpu.VMEM((depth, width), BF16),
            pltpu.VMEM((rows, width), F32),
            pltpu.SemaphoreType.DMA((2, max(1, own.shape[0] // (2 * LANES)))),
        ],
        compiler_params=pltpu.CompilerParams(vmem_limit_bytes=3 * VMEM_BYTES),
        cost_estimate=pl.CostEstimate(
            flops=2 * rows * depth * width, bytes_accessed=2 * depth * width, transcendentals=0
        ),
    )(picked, own, other)
    return [outs[2 * g : 2 * g + 2] for g in range(groups)]


def expert_body(
    block, label, near_a, far_a, near_b, far_b, w_in, w_out_a, w_out_b, *outs
):
    cut, half = near_a.shape
    sums = []
    for g, (near, far) in enumerate(((near_a, far_a), (near_b, far_b))):
        total = jnp.zeros((2 * cut, w_in.shape[1]), F32)
        for c in range(half // CHUNK):
            span = pl.ds(c * CHUNK, CHUNK)
            x = jnp.concatenate([near[:, span], far[:, span]], axis=0)
            w = w_in[pl.ds(g * half + c * CHUNK, CHUNK)]
            total = total + jnp.dot(x, w, preferred_element_type=F32)
        sums.append(total)

    def turn(x):
        q = block
        return jnp.concatenate([x[:q], x[2 * q : 3 * q], x[q : 2 * q], x[3 * q :]], axis=0)

    acts = sums[0] + turn(sums[1])
    hid = acts.shape[1] // 2
    gates, ups = acts[:, :hid], acts[:, hid:]
    inner = gates / (1.0 + jnp.exp(-gates)) * ups
    tails = jnp.concatenate([near_b[:, half:], far_b[:, half:]], axis=0).astype(F32)
    lane = lax.broadcasted_iota(jnp.int32, tails.shape, 1)
    mine = lax.rem(lane, label[1]) == label[0]
    weight = jnp.sum(jnp.where(mine, tails, 0.0), axis=1, keepdims=True)
    for g, w_out in enumerate((w_out_a, w_out_b)):
        send, keep = outs[2 * g : 2 * g + 2]
        x = (inner if g == 0 else turn(inner)).astype(BF16)
        scale = turn(weight) if g == 0 else weight
        for c in range(half // CHUNK):
            span = pl.ds(c * CHUNK, CHUNK)
            y = jnp.dot(x, w_out[:, span], preferred_element_type=F32) * scale
            keep[:, span] = y[:cut]
            send[:, span] = y[cut:].astype(BF16)


def expert(label, tokens, w_in, w_out):
    (near_a, far_a), (near_b, far_b) = tokens
    rows, half = 2 * near_a.shape[0], near_a.shape[1]
    hid = w_out[0].shape[0]
    w_in, *w_out = (pltpu.with_memory_space_constraint(w, pltpu.VMEM) for w in (w_in, *w_out))
    outs = pl.pallas_call(
        functools.partial(expert_body, rows // 4),
        out_shape=projected(rows, half) * 2,
        in_specs=[pl.BlockSpec(memory_space=pltpu.SMEM)] + in_vmem(7),
        out_specs=tuple(in_vmem(4)),
        compiler_params=pltpu.CompilerParams(vmem_limit_bytes=VMEM_BYTES),
        cost_estimate=pl.CostEstimate(
            flops=2 * rows * (w_in.size + 2 * w_out[0].size),
            bytes_accessed=w_in.size + 2 * w_out[0].size,
            transcendentals=rows * hid,
        ),
    )(label, near_a, far_a, near_b, far_b, w_in, *w_out)
    return outs[:2], outs[2:]


def plane_masks(block, planes):
    return block, (planes - block) % planes


def relative_order(first, second, planes, core):
    return np.array(
        [
            plane_masks(z, planes)[core] * SLABS + b * second + a * first
            for a in (0, 1)
            for b in (0, 1)
            for z in range(planes)
        ],
        np.int32,
    )


def on_device(devices):
    planes = devices // SLABS
    chips = devices // 2
    axes = ((AX, AY), (AY, AX))

    def swap(x, mask):
        return lax.ppermute(x, "ep", [(i, i ^ mask) for i in range(devices)])

    def swap_plane(x, block):
        masks = plane_masks(block, planes)
        return lax.ppermute(x, "ep", [(i, i ^ (masks[i % 2] * SLABS)) for i in range(devices)])

    def sum_to_owner(products, rows):
        outs = []
        for g, (send, keep) in enumerate(products):
            x = keep + swap(send, axes[g][0]).astype(F32)
            half = x.shape[0] // 2
            outs.append(x[:half] + swap(x[half:].astype(BF16), axes[g][1]).astype(F32))
        x = jnp.concatenate(outs, axis=1)
        total = x[:rows]
        for d in reversed(range(1, planes)):
            total = total + swap_plane(x[d * rows : (d + 1) * rows].astype(BF16), d).astype(F32)
        return total

    def to_all(x, cut):
        far = [swap_plane(x, d) for d in reversed(range(1, planes))]
        x = jnp.concatenate([x] + far[::-1], axis=0)
        near = [
            jnp.concatenate([part, swap(part, axes[g][1])], axis=0)
            for g, part in enumerate((x[:, :cut], x[:, cut:]))
        ]
        return [(near[g], swap(near[g], axes[g][0])) for g in (0, 1)]

    def body(
        hidden, queries, cache, lengths, value_up, out_proj, norm_gain,
        routes, gates, expert_slot, w_gate, w_up, w_down,
    ):
        rows, width = hidden.shape
        half = width // 2
        me = lax.axis_index("ep")
        core = me % 2
        value_up_other = swap(value_up, CORE)
        out_proj_other = swap(out_proj, CORE)
        w_gate_other, w_up_other, w_down_other = (swap(w, CORE) for w in (w_gate, w_up, w_down))

        latent_out = attend(queries, cache, lengths)
        by_heads = lax.all_to_all(
            latent_out, "ep", split_axis=1, concat_axis=0, tiled=True,
            axis_index_groups=[list(range(c, devices, 2)) for c in (0, 1)],
        )

        even = core == 0
        heads_up = jnp.concatenate(
            [
                jnp.where(even, value_up, value_up_other),
                jnp.where(even, value_up_other, value_up),
            ],
            axis=0,
        )
        by_heads, heads_up, w_gate_other, w_up_other, w_down_other = lax.optimization_barrier(
            (by_heads, heads_up, w_gate_other, w_up_other, w_down_other)
        )

        orders = [
            jnp.where(core == 0, *(jnp.asarray(relative_order(*pair, planes, c)) for c in (0, 1)))
            for pair in axes
        ]
        experts = expert_slot.shape[0]
        labels = jnp.arange(experts, dtype=jnp.int32)
        physical = jnp.sum(
            jnp.where(routes[:, :, None] == labels, expert_slot[None, None, :], 0), axis=2
        )
        weights = jnp.sum(
            jnp.where(physical[:, :, None] == labels, gates[:, :, None], 0.0), axis=1
        )
        pieces = []
        for _ in range(3):
            piece = lax.reduce_precision(weights, 8, 7)
            pieces.append(piece.astype(BF16))
            weights = weights - piece
        tail = jnp.pad(jnp.concatenate(pieces, axis=1), ((0, 0), (0, 128 - 3 * experts)))

        head_values = jnp.einsum(
            "bhl,hlv->bhv", by_heads, heads_up, preferred_element_type=F32
        ).astype(BF16)
        total_rows = head_values.shape[0]
        flat_values = head_values.reshape(total_rows, 2, -1)
        flat_values = jnp.concatenate(
            [
                jnp.where(even, flat_values[:, 0], flat_values[:, 1]),
                jnp.where(even, flat_values[:, 1], flat_values[:, 0]),
            ],
            axis=1,
        )
        picks = []
        for order in orders:
            place = jnp.bitwise_xor(order, me) // 2
            wanted = (place[:, None] * rows + jnp.arange(rows, dtype=jnp.int32)).reshape(-1, 1)
            picks.append(wanted == jnp.arange(total_rows, dtype=jnp.int32)[None, :])
        picks = jnp.concatenate(picks, axis=0).astype(BF16)
        picked = jnp.dot(picks, flat_values, preferred_element_type=F32).astype(BF16)
        products = project_stream(picked.reshape(2, total_rows, -1), out_proj, out_proj_other)
        attended = sum_to_owner(products, rows)
        mixed = hidden.astype(F32) + attended
        scale_rows = lax.rsqrt(jnp.mean(mixed * mixed, axis=1, keepdims=True) + norm_eps)
        normed = (mixed * scale_rows * norm_gain.astype(F32)).astype(BF16)

        w_in, _ = stage_beside((w_gate, w_gate_other, w_up, w_up_other), normed)
        *w_out, _ = stage_columns(w_down, w_down_other, 2, normed)
        tokens = to_all(jnp.concatenate([normed, tail], axis=1), half)
        label = jnp.stack([me // SLABS, jnp.int32(experts)])
        products = expert(label, tokens, w_in, w_out)
        return (mixed + sum_to_owner(products, rows)).astype(BF16)

    return body


def solution(mesh):
    placed = (
        P(("groups", "ep"), None),
        P(("groups", "ep"), None, None),
        P(("groups", "ep"), None, None),
        P(("groups", "ep")),
        P("ep", None, None),
        P("ep", None),
        P(),
        P(("groups", "ep"), None),
        P(("groups", "ep"), None),
        P(),
        P(None, "ep"),
        P(None, "ep"),
        P("ep", None),
    )
    return jax.shard_map(
        on_device(mesh.shape["ep"]),
        mesh=mesh,
        in_specs=placed,
        out_specs=P(("groups", "ep"), None),
        check_vma=False,
    )
```
